32 devices in a mesh: dst: 16 (over z, x, core), tok: 2 (over y).
Axes of the slice: x: 2, y: 2, z: 4, core: 2. Of those that a mesh axis runs over, the one named last changes fastest.
Arguments:
- latents: float32 [2048, 32768], P('tok', 'dst'), may hold values from 0 to 0.2, as said below
- mask: int32 [2048, 32768], P('tok', 'dst'), may hold values from 0 to 1
- errors: bfloat16 [2048, 4, 2048], P('tok'), may hold values from -6 to 6
- decoder: bfloat16 [32768, 4, 2048], P('dst'), may hold values from -0.125 to 0.125
Outputs:
- decoder_grad: bfloat16 [32768, 4, 2048], P('dst', None, 'tok')
- latent_grad: float32 [2048, 32768], P('tok', 'dst')
The draws below stay inside these ranges and needn't reach their ends.
Inputs may be any that keep to these rules, and one draw needn't show every extreme that they name: `latents`: zero exactly where mask is 0 and positive where mask is 1.
All inputs are finite; a program needn't handle non-finite values.
Results may differ from the reference program's by a relative error of at most 0.001.
Values may be sent and summed in bfloat16 or wider, within the bound.
A program may use at most 384 MiB of HBM per device.

```python
import jax
import jax.numpy as jnp
from jax import lax

D = 2048
F = 8192
LAYERS = 4
TOKENS = 2048


def active_pattern(key):
    return jax.random.randint(jax.random.fold_in(key, 7), (TOKENS, LAYERS * F), 0, 2)


def draw_mask(key, part):
    return active_pattern(key).astype(jnp.int32)


def draw_latents(key, part):
    active = active_pattern(key).astype(jnp.float32)
    sub = jax.random.fold_in(key, 11)
    values = jax.random.uniform(sub, (TOKENS, LAYERS * F), jnp.float32, 0.02, 0.14)
    return active * values


def block_levels(own_key, shape, split, smallest, high):
    def one(position, shards_of):
        heights = jax.random.uniform(jax.random.fold_in(jax.random.fold_in(own_key, 6), position), (shards_of,), jnp.float32, smallest / len(split), high / len(split))
        return jnp.repeat(jnp.exp(heights), shape[position] // shards_of).reshape((-1,) + (1,) * (len(shape) - position - 1))

    factor_of = one(*split[0])
    for cut in split[1:]:
        factor_of = factor_of * one(*cut)
    return factor_of


def centred(rng, dims, scale, limit, pieces=(), held_as=jnp.bfloat16):
    values = scale * jax.random.normal(rng, dims, jnp.float32)
    if pieces:
        values = values * block_levels(rng, dims, pieces, -0.22, 0.18)
    return jnp.clip(values, -limit, limit).astype(held_as)


def setup_inputs(seed: int = 0) -> dict:
    key_list = jax.random.split(jax.random.key(seed), 5)
    latents = draw_latents(jax.random.fold_in(key_list[4], 71), 0)
    mask = draw_mask(jax.random.fold_in(key_list[4], 71), 0)
    errors = centred(key_list[2], (TOKENS, LAYERS, D), 1.0, 6.0, ((0, 2),))
    decoder = centred(key_list[3], (LAYERS * F, LAYERS, D), D ** -0.5, 0.125, ((0, 16),))
    return {"latents": latents, "mask": mask, "errors": errors, "decoder": decoder}


def reference(latents, mask, errors, decoder):
    grads = []
    latent_parts = [jnp.zeros((TOKENS, F), jnp.float32) for layer_index in range(LAYERS)]
    for target in range(LAYERS):
        errors_here = errors[:, target, :]
        errors_wide = errors_here.astype(jnp.float32)
        blocks = []
        for distance in range(LAYERS):
            if distance <= target:
                source = target - distance
                chosen = latents[:, source * F:(source + 1) * F]
                blocks.append(jnp.dot(chosen.T, errors_wide, precision=lax.Precision.HIGHEST, preferred_element_type=jnp.float32))
                weights = decoder[target * F:(target + 1) * F, distance, :]
                latent_parts[source] = latent_parts[source] + jnp.dot(errors_here, weights.T, preferred_element_type=jnp.float32)
            else:
                blocks.append(jnp.zeros((F, D), jnp.float32))
        grads.append(jnp.stack(blocks, axis=1).astype(jnp.bfloat16))
    decoder_grad = jnp.concatenate(grads, axis=0)
    latent_grad = mask.astype(jnp.float32) * jnp.concatenate(latent_parts, axis=1)
    return decoder_grad, latent_grad
```

```python
import jax
import jax.numpy as jnp
from jax import lax
from jax.experimental import pallas as pl
from jax.experimental.layout import Layout, with_layout_constraint
from jax.experimental.pallas import tpu as pltpu
from jax.sharding import PartitionSpec as P

LAYERS = 4
CHUNKS = 4
SUM_CHUNKS = 4
TILE = 256
LEVELS = 65535.0
HALF = 32768


def group_shift(array, by, first, last):
    per_group = lax.axis_size("dst") // LAYERS
    pairs = [
        (group * per_group + i, (group + by) * per_group + i)
        for group in range(first, last + 1)
        for i in range(per_group)
    ]
    return lax.ppermute(array, "dst", pairs)


def tok_shift(array, by):
    peers = lax.axis_size("tok")
    return lax.ppermute(array, "tok", [(i, (i + by) % peers) for i in range(peers)])


def after(array, ready):
    return lax.optimization_barrier((array, ready))[0]


def product_kernel(parts, step_ref, *refs):
    total = None
    for part in range(parts):
        code = refs[part][...].astype(jnp.int32) + HALF
        e = refs[parts + part][...]
        for piece in (code & 0xFF00, code & 0xFF):
            exact = piece.astype(jnp.float32).astype(jnp.bfloat16)
            term = jnp.dot(exact, e, preferred_element_type=jnp.float32)
            total = term if total is None else total + term
    refs[2 * parts][...] = (step_ref[...] * total).astype(jnp.bfloat16)


def product(codes, errors, step):
    features, tokens = codes[0].shape
    width = errors[0].shape[1]
    parts = len(codes)
    tile = min(TILE, features)
    return pl.pallas_call(
        lambda *refs: product_kernel(parts, *refs),
        grid=(features // tile,),
        in_specs=[pl.BlockSpec((tile, 1), lambda i: (i, 0))]
        + [pl.BlockSpec((tile, tokens), lambda i: (i, 0))] * parts
        + [pl.BlockSpec((tokens, width), lambda i: (0, 0))] * parts,
        out_specs=pl.BlockSpec((tile, width), lambda i: (i, 0)),
        out_shape=jax.ShapeDtypeStruct((features, width), jnp.bfloat16),
        compiler_params=pltpu.CompilerParams(vmem_limit_bytes=40 * 2**20),
        cost_estimate=pl.CostEstimate(
            flops=4 * parts * features * tokens * width,
            bytes_accessed=2 * (parts * (features * tokens + tokens * width) + features * width),
            transcendentals=0,
        ),
    )(step, *codes, *errors)


def per_device(latents, mask, errors, decoder):
    toks = lax.axis_size("tok")
    tok = lax.axis_index("tok")
    per_group = lax.axis_size("dst") // LAYERS
    place = lax.axis_index("dst")
    my_group = place // per_group
    member = place % per_group
    tokens, _, depth = errors.shape
    features = latents.shape[1]
    width = depth // toks
    rows = tokens // per_group
    members = [list(range(g * per_group, (g + 1) * per_group)) for g in range(LAYERS)]

    peak = jnp.max(latents, axis=0)
    for r in range(1, toks):
        peak = jnp.maximum(peak, tok_shift(peak, r))
    peak = jnp.maximum(peak, 1e-30)
    step = peak * (1.0 / LEVELS)
    per_step = LEVELS / peak

    ahead = LAYERS - 1
    layers = [
        lax.dynamic_index_in_dim(errors, jnp.minimum(my_group + j, LAYERS - 1), 1, keepdims=False)
        for j in range(ahead)
    ]

    own = [lax.dynamic_slice(e, (0, tok * width), (tokens, width)) for e in layers]
    others = []
    for r in range(1, toks):
        to = (tok + r) % toks
        piece = jnp.stack(
            [lax.dynamic_slice(e, (member * rows, to * width), (rows, width)) for e in layers]
        )
        piece = tok_shift(piece, r)
        others.append(lax.all_gather(piece, "dst", axis_index_groups=members, axis=1, tiled=True))
    wide = [[own[j]] + [o[j] for o in others] for j in range(ahead)]

    size = features // CHUNKS
    codes, previous = [], []
    for c in range(CHUNKS):
        columns = slice(c * size, (c + 1) * size)
        scaled = latents[:, columns] * per_step[None, columns] + 0.5
        code = (jnp.minimum(scaled.astype(jnp.int32), 2 * HALF - 1) - HALF).astype(jnp.int16)
        codes.append(code.T)
        previous.append(group_shift(codes[-1], 1, 0, LAYERS - 2))
    step_previous = group_shift(step, 1, 0, LAYERS - 2)

    others_previous = [[tok_shift(p, r) for r in range(1, toks)] for p in previous]
    blocks, ends = [], []
    for c in range(CHUNKS):
        scale = step_previous[c * size:(c + 1) * size, None]
        theirs = [previous[c]] + others_previous[c]
        later = []
        for j in range(ahead - 1, 0, -1):
            sent = product(theirs, wide[j], scale)
            later.append(group_shift(sent, j, 1, LAYERS - 1 - j))
        ends.append(sent)
        blocks.append([product(theirs, wide[0], scale)] + later[::-1])

    bound = 6 * 0.125 * depth * (LAYERS - 1)
    raise_by = 1.0
    while raise_by * 2 * bound < 65504.0:
        raise_by = raise_by * 2
    span = features // SUM_CHUNKS
    sums = [None] * SUM_CHUNKS
    weights = []
    for c in range(SUM_CHUNKS):
        start = after(jnp.int32(c * span), codes[-1])
        part = lax.optimization_barrier(lax.dynamic_slice_in_dim(decoder, start, span, 0))
        weights.append([part[:, k, :] for k in range(LAYERS)])
    for distance in range(LAYERS - 1, -1, -1):
        valid = (distance <= my_group).astype(jnp.float32)
        for c in range(SUM_CHUNKS):
            lhs = layers[0]
            if sums[c] is not None:
                if distance == LAYERS - 2:
                    sums[c] = after(sums[c], ends[(c + 1) * CHUNKS // SUM_CHUNKS - 1])
                lhs = after(lhs, sums[c])
            term = valid * lax.dot_general(
                lhs, weights[c][distance], (((1,), (1,)), ((), ())),
                preferred_element_type=jnp.float32,
            )
            if sums[c] is not None:
                term = term + sums[c].astype(jnp.float32) * (1.0 / raise_by)
            if distance:
                sums[c] = group_shift(
                    (term * raise_by).astype(jnp.float16), -1, distance, LAYERS - 1
                )
            else:
                cut = mask[:, c * span:(c + 1) * span]
                sums[c] = cut.astype(jnp.float32) * term
    latent_grad = jnp.concatenate(sums, axis=1)

    decoder_grad = jnp.zeros((features, LAYERS, width), jnp.bfloat16)
    for c in range(CHUNKS):
        code = after(codes[c], previous[-1])
        mine = [after(codes[c], ends[-1])] + [tok_shift(code, r) for r in range(1, toks)]
        slots = [product(mine, wide[0], step[c * size:(c + 1) * size, None])] + blocks[c]
        block = with_layout_constraint(jnp.stack(slots, axis=1), Layout((0, 1, 2)))
        block = lax.optimization_barrier(block)
        decoder_grad = lax.dynamic_update_slice(decoder_grad, block, (c * size, 0, 0))
    return decoder_grad, latent_grad


def solution(mesh):
    placed = (P("tok", "dst"), P("tok", "dst"), P("tok", None, None), P("dst", None, None))
    return jax.shard_map(
        per_device,
        mesh=mesh,
        in_specs=placed,
        out_specs=(P("dst", None, "tok"), P("tok", "dst")),
        check_vma=False,
    )
```
